256 devices in a mesh: pair: 16 (over x, y), row: 16 (over z, core).
Axes of the slice: x: 4, y: 4, z: 8, core: 2. Of those that a mesh axis runs over, the one named last changes fastest.
Arguments:
- amplitudes: bfloat16 [768, 32, 9216], P(('pair', 'row')), may hold values from -6 to 6
- integrals: bfloat16 [16, 9216, 9216], P('pair', 'row'), may hold values from -0.015625 to 0.015625
- screen: int32 [768, 32], P(('pair', 'row')), may hold values 0 or 1
- live: int32 [32], replicated, may hold values 0 or 1
- owner: int32 [16], replicated, may hold values from 0 to 31, as said below
Outputs:
- ladder: bfloat16 [768, 9216], P(('pair', 'row'))
The draws below stay inside these ranges and needn't reach their ends.
Inputs may be any that keep to these rules, and one draw needn't show every extreme that they name: `owner`: the 16 entries are distinct.
All inputs are finite; a program needn't handle non-finite values. No bound on the sum of `screen` on one device may be relied on, other than what follows from the above.
Results may differ from the reference program's by a relative error of at most 0.0012.
Values may be sent and summed in bfloat16 or wider, within the bound.
No kernel may reach another device: no remote copies, remote signals or barrier semaphores. Data moves between devices by JAX's collectives and lax.ppermute only.
A program may use at most 128 MiB of HBM per device.

```python
import jax
import jax.numpy as jnp
from jax import lax

TT = 9216
OP = 768
K = 16
KA = 32


def draw_owner(key, part):
    key = jax.random.fold_in(key, 11)
    first_key, second_key = jax.random.split(key)
    middle = 1 + jax.random.permutation(first_key, KA - 2)[:K - 2]
    chosen = jnp.concatenate([jnp.array([0, KA - 1], jnp.int32), middle.astype(jnp.int32)])
    return jax.random.permutation(second_key, chosen).astype(jnp.int32)


def with_ends(entries, stream_key, smallest, largest):
    shape = entries.shape
    index_at = [jax.random.randint(jax.random.fold_in(stream_key, axis), (), 0, shape[axis]) for axis in range(len(shape))]
    entries = entries.at[tuple(index_at)].set(smallest)
    longest = shape.index(max(shape))
    index_at[longest] = (index_at[longest] + 1) % shape[longest]
    return entries.at[tuple(index_at)].set(largest)


def levels(stream_key, dims, pieces, least, high):
    def one(axis_at, blocks):
        draws = jax.random.uniform(jax.random.fold_in(jax.random.fold_in(stream_key, 6), axis_at), (blocks,), jnp.float32, least / len(pieces), high / len(pieces))
        return jnp.repeat(jnp.exp(draws), dims[axis_at] // blocks).reshape((-1,) + (1,) * (len(dims) - axis_at - 1))

    factor_of = one(*pieces[0])
    for cut in pieces[1:]:
        factor_of = factor_of * one(*cut)
    return factor_of


def noise(stream_key, extent, width, bound, cuts=(), held_as=jnp.bfloat16):
    result = width * jax.random.normal(stream_key, extent, jnp.float32)
    if cuts:
        result = result * levels(stream_key, extent, cuts, -0.22, 0.18)
    return jnp.clip(result, -bound, bound).astype(held_as)


def setup_inputs(seed: int = 0) -> dict:
    seeds = jax.random.split(jax.random.key(seed), 6)
    return {
        "amplitudes": noise(seeds[0], (OP, KA, TT), 1.0, 6.0, ((0, 256),)),
        "integrals": noise(seeds[1], (K, TT, TT), (TT * K) ** -0.5, 0.015625, ((0, 16), (1, 16))),
        "screen": with_ends((jax.random.randint(seeds[2], (OP, KA), 0, 4) < 3).astype(jnp.int32), jax.random.fold_in(seeds[2], 1), 0, 1),
        "live": with_ends((jax.random.randint(seeds[3], (KA,), 0, 4) < 3).astype(jnp.int32), jax.random.fold_in(seeds[3], 1), 0, 1),
        "owner": draw_owner(jax.random.fold_in(seeds[5], 71), 0),
    }


def reference(amplitudes, integrals, screen, live, owner):
    kept = (screen * live[None, :]).astype(jnp.bfloat16)
    masked = amplitudes * kept[:, :, None]
    ordered = jnp.take(masked, owner.astype(jnp.int32), axis=1)
    total = jnp.zeros((ordered.shape[0], integrals.shape[1]), jnp.float32)
    for slot in range(K):
        total = total + lax.dot_general(ordered[:, slot, :], integrals[slot], (((1,), (1,)), ((), ())), preferred_element_type=jnp.float32)
    return total.astype(jnp.bfloat16)
```

```python
import functools
import math

import jax
import jax.numpy as jnp
from jax import lax
from jax.experimental import pallas as pl
from jax.experimental.pallas import tpu as pltpu
from jax.sharding import PartitionSpec as P

LANES = 128
CUT = 384
THIRDS = 3
STEP = 1536

VMEM = pl.BlockSpec(memory_space=pltpu.VMEM)
SMEM = pl.BlockSpec(memory_space=pltpu.SMEM)
ANY = pl.BlockSpec(memory_space=pl.ANY)


def pick_kernel(owner_hbm, amp_hbm, screen_hbm, live_hbm, out_ref, owner_ref, amp_ref, screen_ref, live_ref, packed, sems):
    slots = out_ref.shape[0]
    own, tiles, width = amp_ref.shape
    cuts = width // CUT
    small = [
        pltpu.make_async_copy(source, target, sems.at[i])
        for i, (source, target) in enumerate(
            ((owner_hbm, owner_ref), (screen_hbm, screen_ref), (live_hbm, live_ref))
        )
    ]
    large = [pltpu.make_async_copy(amp_hbm.at[r], amp_ref.at[r], sems.at[len(small) + r]) for r in range(own)]
    for copy in small + large:
        copy.start()
    for copy in small:
        copy.wait()
    slot = lax.broadcasted_iota(jnp.int32, (slots, tiles), 0)
    tile = lax.broadcasted_iota(jnp.int32, (slots, tiles), 1)
    wanted = jnp.zeros((slots, tiles), jnp.int32)
    for s in range(slots):
        wanted = jnp.where(slot == s, owner_ref[s], wanted)
    for r in range(own):
        kept = screen_ref[r : r + 1, :] * live_ref[...]
        chosen = jnp.where(wanted == tile, kept, 0).astype(jnp.float32).astype(jnp.bfloat16)
        large[r].wait()
        row = jnp.dot(chosen, amp_ref[r], preferred_element_type=jnp.float32)
        for q in range(cuts):
            for t in range(CUT // LANES):
                at = q * CUT + t * LANES
                packed[t, pl.ds(r * cuts + q, slots, stride=own * cuts), :] = row[:, at : at + LANES]
    for s in range(slots):
        for t in range(CUT // LANES):
            lines = packed[t, s * own * cuts : (s + 1) * own * cuts, :]
            out_ref[s, :, t * LANES : (t + 1) * LANES] = lines.astype(out_ref.dtype)


def pick(amplitudes, screen, live, owner):
    own, tiles, width = amplitudes.shape
    slots = owner.shape[0]
    lines = own * width // CUT
    return pl.pallas_call(
        pick_kernel,
        out_shape=jax.ShapeDtypeStruct((slots, lines, CUT), jnp.bfloat16),
        in_specs=[ANY] * 4,
        out_specs=VMEM,
        scratch_shapes=[
            pltpu.SMEM((slots,), jnp.int32),
            pltpu.VMEM(amplitudes.shape, amplitudes.dtype),
            pltpu.VMEM(screen.shape, jnp.int32),
            pltpu.VMEM((1, tiles), jnp.int32),
            pltpu.VMEM((CUT // LANES, slots * lines, LANES), jnp.float32),
            pltpu.SemaphoreType.DMA((3 + own,)),
        ],
        compiler_params=pltpu.CompilerParams(vmem_limit_bytes=56 << 20),
        name="pick",
    )(owner, amplitudes, screen, live.reshape(1, tiles))


def unpack_kernel(own, in_ref, *refs):
    out_refs, packed = refs[:-1], refs[-1]
    group, lines, _ = in_ref.shape
    cuts = lines // own
    each = cuts // len(out_refs)
    for s in range(group):
        for t in range(CUT // LANES):
            packed[t, s * lines : (s + 1) * lines, :] = in_ref[s, :, t * LANES : (t + 1) * LANES].astype(jnp.float32)
    for k, out_ref in enumerate(out_refs):
        for i in range(each):
            for t in range(CUT // LANES):
                rows = [packed[t, pl.ds(r * cuts + k * each + i, group, stride=lines), :] for r in range(own)]
                at = i * CUT + t * LANES
                out_ref[:, at : at + LANES] = jnp.concatenate(rows, axis=0).astype(out_ref.dtype)


def unpack(packed, own):
    group, lines, _ = packed.shape
    out = jax.ShapeDtypeStruct((own * group, lines // own * CUT // THIRDS), packed.dtype)
    return pl.pallas_call(
        functools.partial(unpack_kernel, own),
        out_shape=[out] * THIRDS,
        in_specs=[VMEM],
        out_specs=[VMEM] * THIRDS,
        scratch_shapes=[pltpu.VMEM((CUT // LANES, group * lines, LANES), jnp.float32)],
        compiler_params=pltpu.CompilerParams(vmem_limit_bytes=24 << 20),
        name="unpack",
    )(packed)


def stage_kernel(first, core_ref, mine_ref, theirs_ref, out_ref, token_ref, sems):
    columns, width = mine_ref.shape[0], out_ref.shape[1]
    at = pl.multiple_of(core_ref[0] * columns, columns)
    other = pl.multiple_of((1 - core_ref[0]) * columns, columns)
    part = pl.ds(first, width)
    one = pltpu.make_async_copy(mine_ref.at[:, part], out_ref.at[pl.ds(at, columns)], sems.at[0])
    two = pltpu.make_async_copy(theirs_ref.at[:, part], out_ref.at[pl.ds(other, columns)], sems.at[1])
    one.start()
    two.start()
    token_ref[...] = jnp.zeros_like(token_ref)
    one.wait()
    two.wait()


def stage(core, mine, theirs, k):
    columns, width = mine.shape
    each = width // THIRDS
    return pl.pallas_call(
        functools.partial(stage_kernel, k * each),
        out_shape=[pltpu.VMEM((2 * columns, each), mine.dtype), jax.ShapeDtypeStruct((8, LANES), jnp.float32)],
        in_specs=[SMEM, ANY, ANY],
        out_specs=[VMEM, VMEM],
        scratch_shapes=[pltpu.SemaphoreType.DMA((2,))],
        compiler_params=pltpu.CompilerParams(vmem_limit_bytes=38 << 20),
        cost_estimate=pl.CostEstimate(flops=0, bytes_accessed=4 * columns * each, transcendentals=0),
        name=f"stage{k}",
    )(core, mine, theirs)


def product_kernel(plan, group, side, *refs):
    final = group is not None
    outs = side if final else 1
    operands = 1 + max(max(line) for line in plan)
    a_refs = refs[:operands]
    tile_ref = refs[operands]
    rest = refs[operands + 1 :]
    sorting = 1 if final else 0
    at_ref, rest = (rest[0], rest[1:]) if final else (None, rest)
    scratch = 2 + sorting
    carried = rest[: len(rest) - outs - scratch]
    out_refs = rest[len(carried) : len(carried) + outs]
    rows, total = rest[len(carried) + outs :][:2]
    at = pl.program_id(0)
    high = rows.shape[0] // len(plan)

    for step in range(len(plan[0])):

        @pl.when(at == step)
        def _(step=step):
            for o, line in enumerate(plan):
                rows[o * high : (o + 1) * high, :] = a_refs[line[step]][...]

    def add(columns):
        return lax.dot_general(
            rows[...], tile_ref[:, columns], (((1,), (1,)), ((), ())), preferred_element_type=jnp.float32
        )

    columns = pl.ds(pl.multiple_of(at * STEP, STEP), STEP)

    @pl.when(at == 0)
    def _():
        total[...] = carried[0][...] + add(columns) if carried else add(columns)

    @pl.when(at > 0)
    def _():
        total[...] += add(columns)

    @pl.when(at == pl.num_programs(0) - 1)
    def _():
        if not final:
            out_refs[0][...] = total[...]
            return
        ordered = rest[-1]
        pieces = total.shape[0] // group
        height = ordered.shape[0] // group
        used = pieces * total.shape[1] // LANES
        for q in range(group):
            if used < height:
                ordered[q * height + used : (q + 1) * height, :] = jnp.zeros((height - used, LANES), jnp.float32)
        for t in range(total.shape[1] // LANES):
            for j in range(pieces):
                ordered[pl.ds(t * pieces + j, group, stride=height), :] = total[
                    j * group : (j + 1) * group, t * LANES : (t + 1) * LANES
                ]
        block = ordered.shape[0] // side
        for d, out_ref in enumerate(out_refs):
            to = lax.rem(at_ref[0] + d, side)
            out_ref[...] = ordered[pl.ds(pl.multiple_of(to * block, block), block), :]


def padded(lines):
    return -(-lines // 8) * 8


def product(lines, tiles, carried=None, ends=None):
    operands, blocks, plan = [], [], []
    for line in lines:
        plan.append([])
        for step, (array, block) in enumerate(line):
            known = [i for i, other in enumerate(operands) if other is array]
            if known:
                blocks[known[0]][step] = block
            else:
                operands.append(array)
                blocks.append({step: block})
            plan[-1].append(known[0] if known else len(operands) - 1)
    high = operands[0].shape[0]
    steps = len(plan[0])
    columns = tiles.shape[0]
    rows = high * len(lines)

    def spec(used):
        low, top = min(used), max(used)
        base = used[low]
        return pl.BlockSpec((high, STEP), lambda s: (0, base + jnp.clip(s, low, top) - low))

    extra, specs = [], []
    group, side = None, None
    scratch = [pltpu.VMEM((rows, STEP), jnp.bfloat16), pltpu.VMEM((rows, columns), jnp.float32)]
    if ends is None:
        out, outs = (rows, columns), 1
    else:
        group, side, at = ends
        height = padded(rows // group * columns // LANES)
        out, outs = (group // side * height, LANES), side
        extra.append(at)
        specs.append(SMEM)
        scratch.append(pltpu.VMEM((group * height, LANES), jnp.float32))
    if carried is not None:
        extra.append(carried)
        specs.append(VMEM)
    made = pl.pallas_call(
        functools.partial(product_kernel, plan, group, side),
        grid=(steps,),
        out_shape=[jax.ShapeDtypeStruct(out, jnp.float32)] * outs,
        in_specs=[spec(used) for used in blocks] + [VMEM] + specs,
        out_specs=[pl.BlockSpec(out, lambda s: (0, 0))] * outs,
        scratch_shapes=scratch,
        compiler_params=pltpu.CompilerParams(vmem_limit_bytes=12 << 20),
        cost_estimate=pl.CostEstimate(
            flops=4 * rows * columns * STEP * steps, bytes_accessed=4 << 20, transcendentals=0
        ),
        name=f"product{len(lines)}",
    )(*operands, tiles, *extra)
    return made[0] if ends is None else made


def middle_kernel(side, at_ref, *refs):
    in_refs, out_refs, total = refs[:side], refs[side : 2 * side], refs[-1]
    summed = in_refs[0][...]
    for ref in in_refs[1:]:
        summed = summed + ref[...]
    total[...] = summed
    block = total.shape[0] // side
    for d, out_ref in enumerate(out_refs):
        to = lax.rem(at_ref[0] + d, side)
        out_ref[...] = total[pl.ds(pl.multiple_of(to * block, block), block), :]


def middle(at, parts):
    side = len(parts)
    high = parts[0].shape[0]
    return pl.pallas_call(
        functools.partial(middle_kernel, side),
        out_shape=[jax.ShapeDtypeStruct((high // side, LANES), jnp.float32)] * side,
        in_specs=[SMEM] + [VMEM] * side,
        out_specs=[VMEM] * side,
        scratch_shapes=[pltpu.VMEM((high, LANES), jnp.float32)],
        compiler_params=pltpu.CompilerParams(vmem_limit_bytes=12 << 20),
        name=f"middle{high}",
    )(at, *parts)


def total_kernel(own, side, *refs):
    in_refs, out_refs = refs[:side], refs[side:]
    total = in_refs[0][...]
    for ref in in_refs[1:]:
        total = total + ref[...]
    pieces = own * len(out_refs)
    for o, out_ref in enumerate(out_refs):
        for t in range(out_ref.shape[1] // LANES):
            at = t * pieces + o * own
            out_ref[:, t * LANES : (t + 1) * LANES] = total[at : at + own, :]


def totals(parts, own, origins, width):
    return pl.pallas_call(
        functools.partial(total_kernel, own, len(parts)),
        out_shape=[jax.ShapeDtypeStruct((own, width), jnp.float32)] * origins,
        in_specs=[VMEM] * len(parts),
        out_specs=[VMEM] * origins,
        compiler_params=pltpu.CompilerParams(vmem_limit_bytes=12 << 20),
        name=f"totals{origins}",
    )(*parts)


def place_kernel(offsets, chip_ref, *refs):
    out_ref = refs[-1]
    count = len(offsets)
    for offset, ref in zip(offsets, refs[:-1]):
        width = ref.shape[1]
        source = lax.rem(chip_ref[0] + offset, count)
        at = pl.multiple_of(source * width, LANES)
        out_ref[:, pl.ds(at, width)] = ref[...].astype(out_ref.dtype)


def place(chip, pieces):
    offsets = sorted(pieces)
    own, width = pieces[0].shape
    return pl.pallas_call(
        functools.partial(place_kernel, offsets),
        out_shape=jax.ShapeDtypeStruct((own, width * len(offsets)), jnp.bfloat16),
        in_specs=[SMEM] + [VMEM] * len(offsets),
        out_specs=VMEM,
        compiler_params=pltpu.CompilerParams(vmem_limit_bytes=12 << 20),
        name="place",
    )(chip, *[pieces[o] for o in offsets])


def after(x, *done):
    return lax.optimization_barrier((x,) + done)[0]


def local(amplitudes, integrals, screen, live, owner):
    own = amplitudes.shape[0]
    row_count = lax.axis_size("row")
    pairs = lax.axis_size("pair")
    chips = row_count // 2
    last = chips // 2
    row = lax.axis_index("row").astype(jnp.int32)
    core, chip = (row % 2).reshape(1), (row // 2).reshape(1)
    side = math.isqrt(pairs)
    pair = lax.axis_index("pair").astype(jnp.int32)
    pair_x, pair_y = (pair // side).reshape(1), (pair % side).reshape(1)

    def along(x, d):
        return lax.ppermute(x, "row", [(2 * z + c, 2 * ((z + d) % chips) + c) for z in range(chips) for c in range(2)])

    def exchange(x):
        return lax.all_to_all(x, "pair", split_axis=0, concat_axis=0, tiled=True)

    def shifted(x, dx, dy):
        at = [(i, (i // side + dx) % side * side + (i % side + dy) % side) for i in range(pairs)]
        return lax.ppermute(x, "pair", at)

    def reduce(parts):
        parts = [parts[0]] + [shifted(parts[d], d, 0) for d in range(1, side)]
        parts = middle(pair_y, parts)
        return [parts[0]] + [shifted(parts[d], 0, d) for d in range(1, side)], parts[0]

    mine = integrals[0]
    theirs = lax.ppermute(mine, "row", [(r, r ^ 1) for r in range(row_count)])
    start = unpack(exchange(pick(amplitudes, screen, live, owner)), own)
    theirs, core, chip, pair_x, pair_y = lax.optimization_barrier((theirs, core, chip, pair_x, pair_y))
    tiles, tokens = zip(*[stage(core, mine, theirs, k) for k in range(THIRDS)])

    per = start[0].shape[1] // STEP
    columns = tiles[0].shape[0]
    half = per // 2 * STEP
    forward, backward = list(start), list(start)
    returned = {}

    def whole(array):
        return [(array, b) for b in range(per)]

    def on(k, *done):
        forward[k] = along(after(forward[k], *done) if done else forward[k], 1)
        backward[k] = along(after(backward[k], *done) if done else backward[k], -1)

    def send_back(sums, steps):
        for step, total in zip(steps, sums):
            returned[step % chips] = along(total, step) if step else total

    def chain(k, lines, carried):
        return product(lines, tiles[k], carried, (pairs, side, pair_x) if k == THIRDS - 1 else None)

    near, made = [[whole(start[k])] for k in range(THIRDS)], []
    for hop in range(1, last - 1):
        for k in range(THIRDS):
            on(k, *([tokens[k]] if hop == last - 2 else []))
            near[k] += [whole(forward[k]), whole(backward[k])]
    for k in range(THIRDS):
        made.append(chain(k, near[k], made[-1] if made else None))
    on(0)
    on(1, made[0])
    on(2, made[1])
    parts, tied = reduce(made[-1])
    near_steps = [0] + [d for hop in range(1, last - 1) for d in (-hop, hop)]
    sums = totals(parts, own, len(near_steps), columns)
    far, ended = [], None
    for k, done in enumerate((made[-1][0], tied, sums[0])):
        low = along(after(forward[k][:, :half], done), 1)
        high = along(after(backward[k][:, half:], done), -1)
        far.append([whole(forward[k]), whole(backward[k]), [(low, 0), (high, 0)]])
    send_back(sums, near_steps)
    for k in range(THIRDS):
        if k == 1:
            ended = after(ended, *returned.values())
        ended = chain(k, far[k], ended)
    parts, _ = reduce(ended)
    far_steps = [1 - last, last - 1, last]
    send_back(totals(parts, own, len(far_steps), columns), far_steps)
    return place(chip, {(-step) % chips: piece for step, piece in returned.items()})


def solution(mesh):
    return jax.shard_map(
        local,
        mesh=mesh,
        in_specs=(
            P(("pair", "row"), None, None),
            P("pair", "row", None),
            P(("pair", "row"), None),
            P(),
            P(),
        ),
        out_specs=P(("pair", "row"), None),
        check_vma=False,
    )
```

```python
import functools
import math

import jax
import jax.numpy as jnp
from jax import lax
from jax.experimental import pallas as pl
from jax.experimental.pallas import tpu as pltpu
from jax.sharding import PartitionSpec as P

LANES = 128
CUT = 384
PARTS = 2
STEP = 2304

VMEM = pl.BlockSpec(memory_space=pltpu.VMEM)
SMEM = pl.BlockSpec(memory_space=pltpu.SMEM)
ANY = pl.BlockSpec(memory_space=pl.ANY)
SMALL = pl.CostEstimate(flops=1, bytes_accessed=1, transcendentals=0)


def pick_kernel(owner_hbm, amp_hbm, screen_hbm, live_hbm, out_ref, owner_ref, amp_ref, screen_ref, live_ref, packed, sems):
    slots = out_ref.shape[0]
    own, tiles, width = amp_ref.shape
    cuts = width // CUT
    small = [
        pltpu.make_async_copy(source, target, sems.at[i])
        for i, (source, target) in enumerate(
            ((owner_hbm, owner_ref), (screen_hbm, screen_ref), (live_hbm, live_ref))
        )
    ]
    large = [pltpu.make_async_copy(amp_hbm.at[r], amp_ref.at[r], sems.at[len(small) + r]) for r in range(own)]
    for copy in small + large:
        copy.start()
    for copy in small:
        copy.wait()
    slot = lax.broadcasted_iota(jnp.int32, (slots, tiles), 0)
    tile = lax.broadcasted_iota(jnp.int32, (slots, tiles), 1)
    wanted = jnp.zeros((slots, tiles), jnp.int32)
    for s in range(slots):
        wanted = jnp.where(slot == s, owner_ref[s], wanted)
    for r in range(own):
        kept = screen_ref[r : r + 1, :] * live_ref[...]
        chosen = jnp.where(wanted == tile, kept, 0).astype(jnp.float32).astype(jnp.bfloat16)
        large[r].wait()
        row = jnp.dot(chosen, amp_ref[r], preferred_element_type=jnp.float32)
        for q in range(cuts):
            for t in range(CUT // LANES):
                at = q * CUT + t * LANES
                packed[t, pl.ds(r * cuts + q, slots, stride=own * cuts), :] = row[:, at : at + LANES]
    for s in range(slots):
        for t in range(CUT // LANES):
            lines = packed[t, s * own * cuts : (s + 1) * own * cuts, :]
            out_ref[s, :, t * LANES : (t + 1) * LANES] = lines.astype(out_ref.dtype)


def pick(amplitudes, screen, live, owner):
    own, tiles, width = amplitudes.shape
    slots = owner.shape[0]
    lines = own * width // CUT
    return pl.pallas_call(
        pick_kernel,
        out_shape=jax.ShapeDtypeStruct((slots, lines, CUT), jnp.bfloat16),
        in_specs=[ANY] * 4,
        out_specs=VMEM,
        scratch_shapes=[
            pltpu.SMEM((slots,), jnp.int32),
            pltpu.VMEM(amplitudes.shape, amplitudes.dtype),
            pltpu.VMEM(screen.shape, jnp.int32),
            pltpu.VMEM((1, tiles), jnp.int32),
            pltpu.VMEM((CUT // LANES, slots * lines, LANES), jnp.float32),
            pltpu.SemaphoreType.DMA((3 + own,)),
        ],
        compiler_params=pltpu.CompilerParams(vmem_limit_bytes=16 << 20),
        name="pick",
    )(*[pltpu.with_memory_space_constraint(x, pltpu.HBM) for x in (owner, amplitudes, screen, live.reshape(1, tiles))])


def unpack_kernel(own, core_ref, in_ref, *refs):
    out_refs, packed = refs[:-1], refs[-1]
    group, lines, _ = in_ref.shape
    cuts = lines // own
    each = cuts // len(out_refs)
    side = math.isqrt(group)
    for s in range(group):
        to = jnp.where(core_ref[0] == 0, s, s % side * side + s // side)
        into = pl.ds(pl.multiple_of(to * lines, 8), lines)
        for t in range(CUT // LANES):
            packed[t, into, :] = in_ref[s, :, t * LANES : (t + 1) * LANES].astype(jnp.float32)
    for k, out_ref in enumerate(out_refs):
        for i in range(each):
            for t in range(CUT // LANES):
                rows = [packed[t, pl.ds(r * cuts + k * each + i, group, stride=lines), :] for r in range(own)]
                at = i * CUT + t * LANES
                out_ref[:, at : at + LANES] = jnp.concatenate(rows, axis=0).astype(out_ref.dtype)


def unpack(core, packed, own):
    group, lines, _ = packed.shape
    out = jax.ShapeDtypeStruct((own * group, lines // own * CUT // PARTS), packed.dtype)
    return pl.pallas_call(
        functools.partial(unpack_kernel, own),
        out_shape=[out] * PARTS,
        in_specs=[SMEM, VMEM],
        out_specs=[VMEM] * PARTS,
        scratch_shapes=[pltpu.VMEM((CUT // LANES, group * lines, LANES), jnp.float32)],
        compiler_params=pltpu.CompilerParams(vmem_limit_bytes=24 << 20),
        name="unpack",
    )(core, packed)


def stage_kernel(first, core_ref, mine_ref, theirs_ref, out_ref, token_ref, sems):
    columns, width = mine_ref.shape[0], out_ref.shape[1]
    at = pl.multiple_of(core_ref[0] * columns, columns)
    other = pl.multiple_of((1 - core_ref[0]) * columns, columns)
    part = pl.ds(first, width)
    one = pltpu.make_async_copy(mine_ref.at[:, part], out_ref.at[pl.ds(at, columns)], sems.at[0])
    two = pltpu.make_async_copy(theirs_ref.at[:, part], out_ref.at[pl.ds(other, columns)], sems.at[1])
    one.start()
    two.start()
    token_ref[...] = jnp.zeros_like(token_ref)
    one.wait()
    two.wait()


def stage(core, mine, theirs, k):
    columns, width = mine.shape
    each = width // PARTS
    return pl.pallas_call(
        functools.partial(stage_kernel, k * each),
        out_shape=[pltpu.VMEM((2 * columns, each), mine.dtype), jax.ShapeDtypeStruct((8, LANES), jnp.float32)],
        in_specs=[SMEM, ANY, ANY],
        out_specs=[VMEM, VMEM],
        scratch_shapes=[pltpu.SemaphoreType.DMA((2,))],
        compiler_params=pltpu.CompilerParams(vmem_limit_bytes=2 << 20),
        cost_estimate=SMALL,
        name=f"stage{k}",
    )(core, pltpu.with_memory_space_constraint(mine, pltpu.HBM), pltpu.with_memory_space_constraint(theirs, pltpu.HBM))


def product_kernel(plan, group, side, *refs):
    final = group is not None
    outs = side if final else 1
    operands = 1 + max(max(line) for line in plan)
    a_refs = refs[:operands]
    tile_ref = refs[operands]
    rest = refs[operands + 1 :]
    sorting = 1 if final else 0
    at_ref, rest = (rest[0], rest[1:]) if final else (None, rest)
    scratch = 2 + sorting
    carried = rest[: len(rest) - outs - scratch]
    out_refs = rest[len(carried) : len(carried) + outs]
    rows, total = rest[len(carried) + outs :][:2]
    at = pl.program_id(0)
    high = rows.shape[0] // len(plan)

    for step in range(len(plan[0])):

        @pl.when(at == step)
        def _(step=step):
            for o, line in enumerate(plan):
                rows[o * high : (o + 1) * high, :] = a_refs[line[step]][...]

    def add(columns):
        return lax.dot_general(
            rows[...], tile_ref[:, columns], (((1,), (1,)), ((), ())), preferred_element_type=jnp.float32
        )

    columns = pl.ds(pl.multiple_of(at * STEP, STEP), STEP)

    @pl.when(at == 0)
    def _():
        total[...] = carried[0][...] + add(columns) if carried else add(columns)

    @pl.when(at > 0)
    def _():
        total[...] += add(columns)

    @pl.when(at == pl.num_programs(0) - 1)
    def _():
        if not final:
            out_refs[0][...] = total[...]
            return
        ordered = rest[-1]
        pieces = total.shape[0] // group
        height = ordered.shape[0] // group
        used = pieces * total.shape[1] // LANES
        for q in range(group):
            if used < height:
                ordered[q * height + used : (q + 1) * height, :] = jnp.zeros((height - used, LANES), jnp.float32)
        for t in range(total.shape[1] // LANES):
            for j in range(pieces):
                ordered[pl.ds(t * pieces + j, group, stride=height), :] = total[
                    j * group : (j + 1) * group, t * LANES : (t + 1) * LANES
                ]
        block = ordered.shape[0] // side
        for d, out_ref in enumerate(out_refs):
            to = lax.rem(at_ref[0] + d, side)
            out_ref[...] = ordered[pl.ds(pl.multiple_of(to * block, block), block), :]


def padded(lines):
    return -(-lines // 8) * 8


def product(lines, tiles, carried=None, ends=None):
    operands, blocks, plan = [], [], []
    for line in lines:
        plan.append([])
        for step, (array, block) in enumerate(line):
            known = [i for i, other in enumerate(operands) if other is array]
            if known:
                blocks[known[0]][step] = block
            else:
                operands.append(array)
                blocks.append({step: block})
            plan[-1].append(known[0] if known else len(operands) - 1)
    high = operands[0].shape[0]
    steps = len(plan[0])
    columns = tiles.shape[0]
    rows = high * len(lines)

    def spec(used):
        low, top = min(used), max(used)
        base = used[low]
        return pl.BlockSpec((high, STEP), lambda s: (0, base + jnp.clip(s, low, top) - low))

    extra, specs = [], []
    group, side = None, None
    scratch = [pltpu.VMEM((rows, STEP), jnp.bfloat16), pltpu.VMEM((rows, columns), jnp.float32)]
    if ends is None:
        out, outs = (rows, columns), 1
    else:
        group, side, at = ends
        height = padded(rows // group * columns // LANES)
        out, outs = (group // side * height, LANES), side
        extra.append(at)
        specs.append(SMEM)
        scratch.append(pltpu.VMEM((group * height, LANES), jnp.float32))
    if carried is not None:
        extra.append(carried)
        specs.append(VMEM)
    made = pl.pallas_call(
        functools.partial(product_kernel, plan, group, side),
        grid=(steps,),
        out_shape=[jax.ShapeDtypeStruct(out, jnp.float32)] * outs,
        in_specs=[spec(used) for used in blocks] + [VMEM] + specs,
        out_specs=[pl.BlockSpec(out, lambda s: (0, 0))] * outs,
        scratch_shapes=scratch,
        compiler_params=pltpu.CompilerParams(vmem_limit_bytes=16 << 20),
        cost_estimate=SMALL,
        name=f"product{len(lines)}",
    )(*operands, tiles, *extra)
    return made[0] if ends is None else made


def middle_kernel(side, sizes, at_ref, *refs):
    in_refs, out_refs, totals = refs[: side * len(sizes)], refs[side * len(sizes) :][:side], refs[-len(sizes) :]
    for i, total in enumerate(totals):
        parts = in_refs[i * side : (i + 1) * side]
        summed = parts[0][...]
        for ref in parts[1:]:
            summed = summed + ref[...]
        total[...] = summed
    for d, out_ref in enumerate(out_refs):
        to = lax.rem(at_ref[0] + d, side)
        base = 0
        for size, total in zip(sizes, totals):
            out_ref[base : base + size, :] = total[pl.ds(pl.multiple_of(to * size, 8), size), :]
            base += size


def middle(at, *groups):
    side = len(groups[0])
    sizes = tuple(parts[0].shape[0] // side for parts in groups)
    flat = [part for parts in groups for part in parts]
    return pl.pallas_call(
        functools.partial(middle_kernel, side, sizes),
        out_shape=[jax.ShapeDtypeStruct((sum(sizes), LANES), jnp.float32)] * side,
        in_specs=[SMEM] + [VMEM] * len(flat),
        out_specs=[VMEM] * side,
        scratch_shapes=[pltpu.VMEM((size * side, LANES), jnp.float32) for size in sizes],
        compiler_params=pltpu.CompilerParams(vmem_limit_bytes=16 << 20),
        cost_estimate=SMALL,
        name="middle",
    )(at, *flat)


def total_kernel(own, side, groups, plan, *refs):
    in_refs, out_refs, total, blocks = refs[:side], refs[side:-2], refs[-2], refs[-1]
    summed = in_refs[0][...]
    for ref in in_refs[1:]:
        summed = summed + ref[...]
    total[...] = summed
    blocks[...] = jnp.zeros_like(blocks)
    base = 0
    for steps, tall in groups:
        pieces = own * len(steps)
        for o, step in enumerate(steps):
            for t in range(tall // pieces):
                at = base + t * pieces + o * own
                blocks[step, t * own : (t + 1) * own, :] = total[at : at + own, :]
        base += tall
    for out_ref, steps in zip(out_refs, plan):
        for i, step in enumerate(steps):
            out_ref[i] = blocks[step].astype(out_ref.dtype)


def totals(parts, own, groups, plan, columns):
    count = sum(len(steps) for steps, _ in groups)
    height = -(-own * columns // LANES // 16) * 16
    return pl.pallas_call(
        functools.partial(total_kernel, own, len(parts), groups, plan),
        out_shape=[jax.ShapeDtypeStruct((len(steps), height, LANES), jnp.bfloat16) for steps in plan],
        in_specs=[VMEM] * len(parts),
        out_specs=[VMEM] * len(plan),
        scratch_shapes=[pltpu.VMEM(parts[0].shape, jnp.float32), pltpu.VMEM((count, height, LANES), jnp.float32)],
        compiler_params=pltpu.CompilerParams(vmem_limit_bytes=16 << 20),
        cost_estimate=SMALL,
        name="totals",
    )(*parts)


def unique(blocks):
    arrays = []
    for array, _ in blocks:
        if not any(array is other for other in arrays):
            arrays.append(array)
    return arrays, [([i for i, other in enumerate(arrays) if other is array][0], at) for array, at in blocks]


def gather_kernel(plan, *refs):
    for i, (n, at) in enumerate(plan):
        refs[-1][i] = refs[n][at]


def gather(blocks):
    arrays, plan = unique(blocks)
    return pl.pallas_call(
        functools.partial(gather_kernel, plan),
        out_shape=jax.ShapeDtypeStruct((len(blocks),) + arrays[0].shape[1:], arrays[0].dtype),
        in_specs=[VMEM] * len(arrays),
        out_specs=VMEM,
        compiler_params=pltpu.CompilerParams(vmem_limit_bytes=16 << 20),
        cost_estimate=SMALL,
        name="gather",
    )(*arrays)


def place_kernel(plan, width, chip_ref, *refs):
    out_ref = refs[-1]
    own, count = out_ref.shape[0], len(plan)
    for step, (n, at) in enumerate(plan):
        source = lax.rem(chip_ref[0] - step + count, count)
        block = refs[n][at].astype(jnp.float32)
        row = [block[t * own : (t + 1) * own, :] for t in range(width // LANES)]
        into = pl.ds(pl.multiple_of(source * width, LANES), width)
        out_ref[:, into] = jnp.concatenate(row, axis=1).astype(out_ref.dtype)


def place(chip, blocks, own, width):
    arrays, plan = unique(blocks)
    return pl.pallas_call(
        functools.partial(place_kernel, plan, width),
        out_shape=jax.ShapeDtypeStruct((own, width * len(blocks)), jnp.bfloat16),
        in_specs=[SMEM] + [VMEM] * len(arrays),
        out_specs=VMEM,
        compiler_params=pltpu.CompilerParams(vmem_limit_bytes=16 << 20),
        cost_estimate=SMALL,
        name="place",
    )(chip, *arrays)


def after(x, *done):
    return lax.optimization_barrier((x,) + done)[0]


def local(amplitudes, integrals, screen, live, owner):
    own = amplitudes.shape[0]
    row_count = lax.axis_size("row")
    pairs = lax.axis_size("pair")
    chips = row_count // 2
    last = chips // 2
    row = lax.axis_index("row").astype(jnp.int32)
    core, chip = (row % 2).reshape(1), (row // 2).reshape(1)
    side = math.isqrt(pairs)
    pair = lax.axis_index("pair").astype(jnp.int32)
    slow = jnp.where(core == 0, pair // side, pair % side)
    fast = jnp.where(core == 0, pair % side, pair // side)

    def along(x, d):
        return lax.ppermute(x, "row", [(2 * z + c, 2 * ((z + d) % chips) + c) for z in range(chips) for c in range(2)])

    def shifted(x, d, slow):
        moves = []
        for p in range(pairs):
            over_x = p % side + (p // side + d) % side * side
            over_y = p // side * side + (p % side + d) % side
            for r in range(row_count):
                to = over_x if (r % 2 == 0) == slow else over_y
                moves.append((p * row_count + r, to * row_count + r))
        return lax.ppermute(x, ("pair", "row"), moves)

    mine = integrals[0]
    theirs = lax.ppermute(mine, "row", [(r, r ^ 1) for r in range(row_count)])
    columns = 2 * mine.shape[0]
    packed, core, chip, slow, fast = lax.optimization_barrier(
        (pick(amplitudes, screen, live, owner), core, chip, slow, fast)
    )
    start = unpack(core, lax.all_to_all(packed, "pair", split_axis=0, concat_axis=0, tiled=True), own)

    tiles, tokens = zip(*[stage(core, mine, theirs, k) for k in range(PARTS)])
    per = start[0].shape[1] // STEP
    half = per // 2 * STEP
    forward, backward = list(start), list(start)

    def whole(array):
        return [(array, b) for b in range(per)]

    def on(k, *done):
        forward[k] = along(after(forward[k], *done) if done else forward[k], 1)
        backward[k] = along(after(backward[k], *done) if done else backward[k], -1)

    def chain(k, lines, carried):
        ends = (pairs, side, slow) if k == PARTS - 1 else None
        return product(lines, tiles[k], carried, ends)

    def over_slow(parts):
        return [parts[0]] + [shifted(parts[d], d, True) for d in range(1, side)]

    def over_fast(parts):
        return [parts[0]] + [shifted(parts[d], d, False) for d in range(1, side)]

    near, made = [[whole(start[k])] for k in range(PARTS)], []
    for hop in range(1, last - 1):
        for k in range(PARTS):
            on(k, *([tokens[k]] if hop == last - 2 else []))
            near[k] += [whole(forward[k]), whole(backward[k])]
    for k in range(PARTS):
        made.append(chain(k, near[k], made[-1] if made else None))
    near_steps = (0,) + tuple(d % chips for hop in range(1, last - 1) for d in (-hop, hop))
    on(0)
    on(1, made[0])
    near_parts = over_slow(made[-1])
    far, ended = [], None
    for k in range(PARTS):
        low = along(after(forward[k][:, :half], made[-1][0]), 1)
        high = along(after(backward[k][:, half:], made[-1][0]), -1)
        far.append([whole(forward[k]), whole(backward[k]), [(low, 0), (high, 0)]])
    for k in range(PARTS):
        if k == PARTS - 1:
            ended = after(ended, *near_parts)
        ended = chain(k, far[k], ended)
    far_steps = ((1 - last) % chips, last - 1, last)
    groups = tuple((steps, padded(own * len(steps) * columns // LANES)) for steps in (near_steps, far_steps))
    plan = (far_steps[::-1], (0,), (1, 2), (chips - 1, chips - 2))
    parts = over_fast(middle(fast, near_parts, over_slow(ended)))
    distant, here, right, left = totals(parts, own, groups, plan, columns)
    distant, right, left = along(distant, last), along(right, 1), along(left, -1)
    right_two = along(gather([(right, 1), (distant, plan[0].index(last + 1))]), 1)
    left_two = along(gather([(left, 1), (distant, plan[0].index(last - 1))]), -1)
    blocks = {
        0: (here, 0),
        1: (right, 0),
        2: (right_two, 0),
        last - 1: (left_two, 1),
        last: (distant, plan[0].index(last)),
        last + 1: (right_two, 1),
        chips - 2: (left_two, 0),
        chips - 1: (left, 0),
    }
    return place(chip, [blocks[s] for s in range(chips)], own, columns)


def solution(mesh):
    return jax.shard_map(
        local,
        mesh=mesh,
        in_specs=(
            P(("pair", "row"), None, None),
            P("pair", "row", None),
            P(("pair", "row"), None),
            P(),
            P(),
        ),
        out_specs=P(("pair", "row"), None),
        check_vma=False,
    )
```

```python
import functools
import math

import jax
import jax.numpy as jnp
from jax import lax
from jax.experimental import pallas as pl
from jax.experimental.pallas import tpu as pltpu
from jax.sharding import PartitionSpec as P

LANES = 128
CUT = 384
PARTS = 3
STEP = 1536

VMEM = pl.BlockSpec(memory_space=pltpu.VMEM)
SMEM = pl.BlockSpec(memory_space=pltpu.SMEM)
ANY = pl.BlockSpec(memory_space=pl.ANY)
SMALL = pl.CostEstimate(flops=1, bytes_accessed=1, transcendentals=0)


def pick_kernel(owner_hbm, amp_hbm, screen_hbm, live_hbm, out_ref, owner_ref, amp_ref, screen_ref, live_ref, packed, sems):
    slots = out_ref.shape[0]
    own, tiles, width = amp_ref.shape
    cuts = width // CUT
    small = [
        pltpu.make_async_copy(source, target, sems.at[i])
        for i, (source, target) in enumerate(
            ((owner_hbm, owner_ref), (screen_hbm, screen_ref), (live_hbm, live_ref))
        )
    ]
    large = [pltpu.make_async_copy(amp_hbm.at[r], amp_ref.at[r], sems.at[len(small) + r]) for r in range(own)]
    for copy in small + large:
        copy.start()
    for copy in small:
        copy.wait()
    slot = lax.broadcasted_iota(jnp.int32, (slots, tiles), 0)
    tile = lax.broadcasted_iota(jnp.int32, (slots, tiles), 1)
    wanted = jnp.zeros((slots, tiles), jnp.int32)
    for s in range(slots):
        wanted = jnp.where(slot == s, owner_ref[s], wanted)
    for r in range(own):
        kept = screen_ref[r : r + 1, :] * live_ref[...]
        chosen = jnp.where(wanted == tile, kept, 0).astype(jnp.float32).astype(jnp.bfloat16)
        large[r].wait()
        row = jnp.dot(chosen, amp_ref[r], preferred_element_type=jnp.float32)
        for q in range(cuts):
            for t in range(CUT // LANES):
                at = q * CUT + t * LANES
                packed[t, pl.ds(r * cuts + q, slots, stride=own * cuts), :] = row[:, at : at + LANES]
    for s in range(slots):
        for t in range(CUT // LANES):
            lines = packed[t, s * own * cuts : (s + 1) * own * cuts, :]
            out_ref[s, :, t * LANES : (t + 1) * LANES] = lines.astype(out_ref.dtype)


def pick(amplitudes, screen, live, owner):
    own, tiles, width = amplitudes.shape
    slots = owner.shape[0]
    lines = own * width // CUT
    return pl.pallas_call(
        pick_kernel,
        out_shape=jax.ShapeDtypeStruct((slots, lines, CUT), jnp.bfloat16),
        in_specs=[ANY] * 4,
        out_specs=VMEM,
        scratch_shapes=[
            pltpu.SMEM((slots,), jnp.int32),
            pltpu.VMEM(amplitudes.shape, amplitudes.dtype),
            pltpu.VMEM(screen.shape, jnp.int32),
            pltpu.VMEM((1, tiles), jnp.int32),
            pltpu.VMEM((CUT // LANES, slots * lines, LANES), jnp.float32),
            pltpu.SemaphoreType.DMA((3 + own,)),
        ],
        compiler_params=pltpu.CompilerParams(vmem_limit_bytes=16 << 20),
        name="pick",
    )(*[pltpu.with_memory_space_constraint(x, pltpu.HBM) for x in (owner, amplitudes, screen, live.reshape(1, tiles))])


def unpack_kernel(own, core_ref, in_ref, *refs):
    out_refs, packed = refs[:-1], refs[-1]
    group, lines, _ = in_ref.shape
    cuts = lines // own
    each = cuts // len(out_refs)
    side = math.isqrt(group)
    for s in range(group):
        to = jnp.where(core_ref[0] == 0, s, s % side * side + s // side)
        into = pl.ds(pl.multiple_of(to * lines, 8), lines)
        for t in range(CUT // LANES):
            packed[t, into, :] = in_ref[s, :, t * LANES : (t + 1) * LANES].astype(jnp.float32)
    for k, out_ref in enumerate(out_refs):
        for i in range(each):
            for t in range(CUT // LANES):
                rows = [packed[t, pl.ds(r * cuts + k * each + i, group, stride=lines), :] for r in range(own)]
                at = i * CUT + t * LANES
                out_ref[:, at : at + LANES] = jnp.concatenate(rows, axis=0).astype(out_ref.dtype)


def unpack(core, packed, own):
    group, lines, _ = packed.shape
    out = jax.ShapeDtypeStruct((own * group, lines // own * CUT // PARTS), packed.dtype)
    return pl.pallas_call(
        functools.partial(unpack_kernel, own),
        out_shape=[out] * PARTS,
        in_specs=[SMEM, VMEM],
        out_specs=[VMEM] * PARTS,
        scratch_shapes=[pltpu.VMEM((CUT // LANES, group * lines, LANES), jnp.float32)],
        compiler_params=pltpu.CompilerParams(vmem_limit_bytes=24 << 20),
        name="unpack",
    )(core, packed)


def stage_kernel(first, core_ref, mine_ref, theirs_ref, out_ref, token_ref, sems):
    columns, width = mine_ref.shape[0], out_ref.shape[1]
    at = pl.multiple_of(core_ref[0] * columns, columns)
    other = pl.multiple_of((1 - core_ref[0]) * columns, columns)
    part = pl.ds(first, width)
    one = pltpu.make_async_copy(mine_ref.at[:, part], out_ref.at[pl.ds(at, columns)], sems.at[0])
    two = pltpu.make_async_copy(theirs_ref.at[:, part], out_ref.at[pl.ds(other, columns)], sems.at[1])
    one.start()
    two.start()
    token_ref[...] = jnp.zeros_like(token_ref)
    one.wait()
    two.wait()


def stage(core, mine, theirs, k):
    columns, width = mine.shape
    each = width // PARTS
    return pl.pallas_call(
        functools.partial(stage_kernel, k * each),
        out_shape=[pltpu.VMEM((2 * columns, each), mine.dtype), jax.ShapeDtypeStruct((8, LANES), jnp.float32)],
        in_specs=[SMEM, ANY, ANY],
        out_specs=[VMEM, VMEM],
        scratch_shapes=[pltpu.SemaphoreType.DMA((2,))],
        compiler_params=pltpu.CompilerParams(vmem_limit_bytes=2 << 20),
        cost_estimate=SMALL,
        name=f"stage{k}",
    )(core, pltpu.with_memory_space_constraint(mine, pltpu.HBM), pltpu.with_memory_space_constraint(theirs, pltpu.HBM))


def product_kernel(plan, group, side, *refs):
    final = group is not None
    outs = side if final else 1
    operands = 1 + max(max(line) for line in plan)
    a_refs = refs[:operands]
    tile_ref = refs[operands]
    rest = refs[operands + 1 :]
    sorting = 1 if final else 0
    at_ref, rest = (rest[0], rest[1:]) if final else (None, rest)
    scratch = 2 + sorting
    carried = rest[: len(rest) - outs - scratch]
    out_refs = rest[len(carried) : len(carried) + outs]
    rows, total = rest[len(carried) + outs :][:2]
    at = pl.program_id(0)
    high = rows.shape[0] // len(plan)

    for step in range(len(plan[0])):

        @pl.when(at == step)
        def _(step=step):
            for o, line in enumerate(plan):
                rows[o * high : (o + 1) * high, :] = a_refs[line[step]][...]

    def add(columns):
        return lax.dot_general(
            rows[...], tile_ref[:, columns], (((1,), (1,)), ((), ())), preferred_element_type=jnp.float32
        )

    columns = pl.ds(pl.multiple_of(at * STEP, STEP), STEP)

    @pl.when(at == 0)
    def _():
        total[...] = carried[0][...] + add(columns) if carried else add(columns)

    @pl.when(at > 0)
    def _():
        total[...] += add(columns)

    @pl.when(at == pl.num_programs(0) - 1)
    def _():
        if not final:
            out_refs[0][...] = total[...]
            return
        ordered = rest[-1]
        pieces = total.shape[0] // group
        height = ordered.shape[0] // group
        used = pieces * total.shape[1] // LANES
        for q in range(group):
            if used < height:
                ordered[q * height + used : (q + 1) * height, :] = jnp.zeros((height - used, LANES), jnp.float32)
        for t in range(total.shape[1] // LANES):
            for j in range(pieces):
                ordered[pl.ds(t * pieces + j, group, stride=height), :] = total[
                    j * group : (j + 1) * group, t * LANES : (t + 1) * LANES
                ]
        block = ordered.shape[0] // side
        for d, out_ref in enumerate(out_refs):
            to = lax.rem(at_ref[0] + d, side)
            out_ref[...] = ordered[pl.ds(pl.multiple_of(to * block, block), block), :]


def padded(lines):
    return -(-lines // 8) * 8


def product(lines, tiles, carried=None, ends=None):
    operands, blocks, plan = [], [], []
    for line in lines:
        plan.append([])
        for step, (array, block) in enumerate(line):
            known = [i for i, other in enumerate(operands) if other is array]
            if known:
                blocks[known[0]][step] = block
            else:
                operands.append(array)
                blocks.append({step: block})
            plan[-1].append(known[0] if known else len(operands) - 1)
    high = operands[0].shape[0]
    steps = len(plan[0])
    columns = tiles.shape[0]
    rows = high * len(lines)

    def spec(used):
        low, top = min(used), max(used)
        base = used[low]
        return pl.BlockSpec((high, STEP), lambda s: (0, base + jnp.clip(s, low, top) - low))

    extra, specs = [], []
    group, side = None, None
    scratch = [pltpu.VMEM((rows, STEP), jnp.bfloat16), pltpu.VMEM((rows, columns), jnp.float32)]
    if ends is None:
        out, outs = (rows, columns), 1
    else:
        group, side, at = ends
        height = padded(rows // group * columns // LANES)
        out, outs = (group // side * height, LANES), side
        extra.append(at)
        specs.append(SMEM)
        scratch.append(pltpu.VMEM((group * height, LANES), jnp.float32))
    if carried is not None:
        extra.append(carried)
        specs.append(VMEM)
    made = pl.pallas_call(
        functools.partial(product_kernel, plan, group, side),
        grid=(steps,),
        out_shape=[jax.ShapeDtypeStruct(out, jnp.float32)] * outs,
        in_specs=[spec(used) for used in blocks] + [VMEM] + specs,
        out_specs=[pl.BlockSpec(out, lambda s: (0, 0))] * outs,
        scratch_shapes=scratch,
        compiler_params=pltpu.CompilerParams(vmem_limit_bytes=16 << 20),
        cost_estimate=SMALL,
        name=f"product{len(lines)}",
    )(*operands, tiles, *extra)
    return made[0] if ends is None else made


def middle_kernel(side, sizes, at_ref, *refs):
    in_refs, out_refs, totals = refs[: side * len(sizes)], refs[side * len(sizes) :][:side], refs[-len(sizes) :]
    for i, total in enumerate(totals):
        parts = in_refs[i * side : (i + 1) * side]
        summed = parts[0][...]
        for ref in parts[1:]:
            summed = summed + ref[...]
        total[...] = summed
    for d, out_ref in enumerate(out_refs):
        to = lax.rem(at_ref[0] + d, side)
        base = 0
        for size, total in zip(sizes, totals):
            out_ref[base : base + size, :] = total[pl.ds(pl.multiple_of(to * size, 8), size), :]
            base += size


def middle(at, *groups):
    side = len(groups[0])
    sizes = tuple(parts[0].shape[0] // side for parts in groups)
    flat = [part for parts in groups for part in parts]
    return pl.pallas_call(
        functools.partial(middle_kernel, side, sizes),
        out_shape=[jax.ShapeDtypeStruct((sum(sizes), LANES), jnp.float32)] * side,
        in_specs=[SMEM] + [VMEM] * len(flat),
        out_specs=[VMEM] * side,
        scratch_shapes=[pltpu.VMEM((size * side, LANES), jnp.float32) for size in sizes],
        compiler_params=pltpu.CompilerParams(vmem_limit_bytes=16 << 20),
        cost_estimate=SMALL,
        name="middle",
    )(at, *flat)


def total_kernel(own, side, groups, plan, *refs):
    in_refs, out_refs, total, blocks = refs[:side], refs[side:-2], refs[-2], refs[-1]
    summed = in_refs[0][...]
    for ref in in_refs[1:]:
        summed = summed + ref[...]
    total[...] = summed
    blocks[...] = jnp.zeros_like(blocks)
    base = 0
    for steps, tall in groups:
        pieces = own * len(steps)
        for o, step in enumerate(steps):
            for t in range(tall // pieces):
                at = base + t * pieces + o * own
                blocks[step, t * own : (t + 1) * own, :] = total[at : at + own, :]
        base += tall
    for out_ref, steps in zip(out_refs, plan):
        for i, step in enumerate(steps):
            out_ref[i] = blocks[step].astype(out_ref.dtype)


def totals(parts, own, groups, plan, columns):
    count = sum(len(steps) for steps, _ in groups)
    height = -(-own * columns // LANES // 16) * 16
    return pl.pallas_call(
        functools.partial(total_kernel, own, len(parts), groups, plan),
        out_shape=[jax.ShapeDtypeStruct((len(steps), height, LANES), jnp.bfloat16) for steps in plan],
        in_specs=[VMEM] * len(parts),
        out_specs=[VMEM] * len(plan),
        scratch_shapes=[pltpu.VMEM(parts[0].shape, jnp.float32), pltpu.VMEM((count, height, LANES), jnp.float32)],
        compiler_params=pltpu.CompilerParams(vmem_limit_bytes=16 << 20),
        cost_estimate=SMALL,
        name="totals",
    )(*parts)


def unique(blocks):
    arrays = []
    for array, _ in blocks:
        if not any(array is other for other in arrays):
            arrays.append(array)
    return arrays, [([i for i, other in enumerate(arrays) if other is array][0], at) for array, at in blocks]


def gather_kernel(plan, *refs):
    for i, (n, at) in enumerate(plan):
        refs[-1][i] = refs[n][at]


def gather(blocks):
    arrays, plan = unique(blocks)
    return pl.pallas_call(
        functools.partial(gather_kernel, plan),
        out_shape=jax.ShapeDtypeStruct((len(blocks),) + arrays[0].shape[1:], arrays[0].dtype),
        in_specs=[VMEM] * len(arrays),
        out_specs=VMEM,
        compiler_params=pltpu.CompilerParams(vmem_limit_bytes=16 << 20),
        cost_estimate=SMALL,
        name="gather",
    )(*arrays)


def place_kernel(plan, width, chip_ref, *refs):
    out_ref = refs[-1]
    own, count = out_ref.shape[0], len(plan)
    for step, (n, at) in enumerate(plan):
        source = lax.rem(chip_ref[0] - step + count, count)
        block = refs[n][at].astype(jnp.float32)
        row = [block[t * own : (t + 1) * own, :] for t in range(width // LANES)]
        into = pl.ds(pl.multiple_of(source * width, LANES), width)
        out_ref[:, into] = jnp.concatenate(row, axis=1).astype(out_ref.dtype)


def place(chip, blocks, own, width):
    arrays, plan = unique(blocks)
    return pl.pallas_call(
        functools.partial(place_kernel, plan, width),
        out_shape=jax.ShapeDtypeStruct((own, width * len(blocks)), jnp.bfloat16),
        in_specs=[SMEM] + [VMEM] * len(arrays),
        out_specs=VMEM,
        compiler_params=pltpu.CompilerParams(vmem_limit_bytes=16 << 20),
        cost_estimate=SMALL,
        name="place",
    )(chip, *arrays)


def after(x, *done):
    return lax.optimization_barrier((x,) + done)[0]


def local(amplitudes, integrals, screen, live, owner):
    own = amplitudes.shape[0]
    row_count = lax.axis_size("row")
    pairs = lax.axis_size("pair")
    chips = row_count // 2
    last = chips // 2
    row = lax.axis_index("row").astype(jnp.int32)
    core, chip = (row % 2).reshape(1), (row // 2).reshape(1)
    side = math.isqrt(pairs)
    pair = lax.axis_index("pair").astype(jnp.int32)
    slow = jnp.where(core == 0, pair // side, pair % side)
    fast = jnp.where(core == 0, pair % side, pair // side)

    def along(x, d):
        return lax.ppermute(x, "row", [(2 * z + c, 2 * ((z + d) % chips) + c) for z in range(chips) for c in range(2)])

    def shifted(x, d, slow):
        moves = []
        for p in range(pairs):
            over_x = p % side + (p // side + d) % side * side
            over_y = p // side * side + (p % side + d) % side
            for r in range(row_count):
                to = over_x if (r % 2 == 0) == slow else over_y
                moves.append((p * row_count + r, to * row_count + r))
        return lax.ppermute(x, ("pair", "row"), moves)

    mine = integrals[0]
    theirs = lax.ppermute(mine, "row", [(r, r ^ 1) for r in range(row_count)])
    columns = 2 * mine.shape[0]
    packed, core, chip, slow, fast = lax.optimization_barrier(
        (pick(amplitudes, screen, live, owner), core, chip, slow, fast)
    )
    start = unpack(core, lax.all_to_all(packed, "pair", split_axis=0, concat_axis=0, tiled=True), own)

    tiles, tokens = zip(*[stage(core, mine, theirs, k) for k in range(PARTS)])
    per = start[0].shape[1] // STEP
    half = per // 2 * STEP
    forward, backward = list(start), list(start)

    def whole(array):
        return [(array, b) for b in range(per)]

    def on(k, *done):
        forward[k] = along(after(forward[k], *done) if done else forward[k], 1)
        backward[k] = along(after(backward[k], *done) if done else backward[k], -1)

    def chain(k, lines, carried):
        ends = (pairs, side, slow) if k == PARTS - 1 else None
        return product(lines, tiles[k], carried, ends)

    def over_slow(parts):
        return [parts[0]] + [shifted(parts[d], d, True) for d in range(1, side)]

    def over_fast(parts):
        return [parts[0]] + [shifted(parts[d], d, False) for d in range(1, side)]

    near, made = [[whole(start[k])] for k in range(PARTS)], []
    for hop in range(1, last - 1):
        for k in range(PARTS):
            on(k, *([tokens[k]] if hop == last - 2 else []))
            near[k] += [whole(forward[k]), whole(backward[k])]
    for k in range(PARTS):
        made.append(chain(k, near[k], made[-1] if made else None))
    near_steps = (0,) + tuple(d % chips for hop in range(1, last - 1) for d in (-hop, hop))
    on(0)
    for k in range(1, PARTS):
        on(k, made[k - 1])
    near_parts = over_slow(made[-1])
    far, ended = [], None
    for k in range(PARTS):
        low = along(after(forward[k][:, :half], made[-1][0]), 1)
        high = along(after(backward[k][:, half:], made[-1][0]), -1)
        far.append([whole(forward[k]), whole(backward[k]), [(low, 0), (high, 0)]])
    for k in range(PARTS):
        if k == PARTS - 1:
            ended = after(ended, *near_parts)
        ended = chain(k, far[k], ended)
    far_steps = ((1 - last) % chips, last - 1, last)
    groups = tuple((steps, padded(own * len(steps) * columns // LANES)) for steps in (near_steps, far_steps))
    plan = (far_steps[::-1], (0,), (1, 2), (chips - 1, chips - 2))
    parts = over_fast(middle(fast, near_parts, over_slow(ended)))
    distant, here, right, left = totals(parts, own, groups, plan, columns)
    distant, right, left = along(distant, last), along(right, 1), along(left, -1)
    right_two = along(gather([(right, 1), (distant, plan[0].index(last + 1))]), 1)
    left_two = along(gather([(left, 1), (distant, plan[0].index(last - 1))]), -1)
    blocks = {
        0: (here, 0),
        1: (right, 0),
        2: (right_two, 0),
        last - 1: (left_two, 1),
        last: (distant, plan[0].index(last)),
        last + 1: (right_two, 1),
        chips - 2: (left_two, 0),
        chips - 1: (left, 0),
    }
    return place(chip, [blocks[s] for s in range(chips)], own, columns)


def solution(mesh):
    return jax.shard_map(
        local,
        mesh=mesh,
        in_specs=(
            P(("pair", "row"), None, None),
            P("pair", "row", None),
            P(("pair", "row"), None),
            P(),
            P(),
        ),
        out_specs=P(("pair", "row"), None),
        check_vma=False,
    )
```

```python
import functools
import math

import jax
import jax.numpy as jnp
from jax import lax
from jax.experimental import pallas as pl
from jax.experimental.pallas import tpu as pltpu
from jax.sharding import PartitionSpec as P

LANES = 128
CUT = 384
PARTS = 2
STEP = 2304

VMEM = pl.BlockSpec(memory_space=pltpu.VMEM)
SMEM = pl.BlockSpec(memory_space=pltpu.SMEM)
ANY = pl.BlockSpec(memory_space=pl.ANY)
SMALL = pl.CostEstimate(flops=1, bytes_accessed=1, transcendentals=0)


def pick_kernel(owner_hbm, amp_hbm, screen_hbm, live_hbm, out_ref, owner_ref, amp_ref, screen_ref, live_ref, packed, sems):
    slots = out_ref.shape[0]
    own, tiles, width = amp_ref.shape
    cuts = width // CUT
    small = [
        pltpu.make_async_copy(source, target, sems.at[i])
        for i, (source, target) in enumerate(
            ((owner_hbm, owner_ref), (screen_hbm, screen_ref), (live_hbm, live_ref))
        )
    ]
    large = [pltpu.make_async_copy(amp_hbm.at[r], amp_ref.at[r], sems.at[len(small) + r]) for r in range(own)]
    for copy in small + large:
        copy.start()
    for copy in small:
        copy.wait()
    slot = lax.broadcasted_iota(jnp.int32, (slots, tiles), 0)
    tile = lax.broadcasted_iota(jnp.int32, (slots, tiles), 1)
    wanted = jnp.zeros((slots, tiles), jnp.int32)
    for s in range(slots):
        wanted = jnp.where(slot == s, owner_ref[s], wanted)
    for r in range(own):
        kept = screen_ref[r : r + 1, :] * live_ref[...]
        chosen = jnp.where(wanted == tile, kept, 0).astype(jnp.float32).astype(jnp.bfloat16)
        large[r].wait()
        row = jnp.dot(chosen, amp_ref[r], preferred_element_type=jnp.float32)
        for q in range(cuts):
            for t in range(CUT // LANES):
                at = q * CUT + t * LANES
                packed[t, pl.ds(r * cuts + q, slots, stride=own * cuts), :] = row[:, at : at + LANES]
    for s in range(slots):
        for t in range(CUT // LANES):
            lines = packed[t, s * own * cuts : (s + 1) * own * cuts, :]
            out_ref[s, :, t * LANES : (t + 1) * LANES] = lines.astype(out_ref.dtype)


def pick(amplitudes, screen, live, owner):
    own, tiles, width = amplitudes.shape
    slots = owner.shape[0]
    lines = own * width // CUT
    return pl.pallas_call(
        pick_kernel,
        out_shape=jax.ShapeDtypeStruct((slots, lines, CUT), jnp.bfloat16),
        in_specs=[ANY] * 4,
        out_specs=VMEM,
        scratch_shapes=[
            pltpu.SMEM((slots,), jnp.int32),
            pltpu.VMEM(amplitudes.shape, amplitudes.dtype),
            pltpu.VMEM(screen.shape, jnp.int32),
            pltpu.VMEM((1, tiles), jnp.int32),
            pltpu.VMEM((CUT // LANES, slots * lines, LANES), jnp.float32),
            pltpu.SemaphoreType.DMA((3 + own,)),
        ],
        compiler_params=pltpu.CompilerParams(vmem_limit_bytes=16 << 20),
        name="pick",
    )(*[pltpu.with_memory_space_constraint(x, pltpu.HBM) for x in (owner, amplitudes, screen, live.reshape(1, tiles))])


def unpack_kernel(own, core_ref, in_ref, *refs):
    out_refs, packed = refs[:-1], refs[-1]
    group, lines, _ = in_ref.shape
    cuts = lines // own
    each = cuts // len(out_refs)
    side = math.isqrt(group)
    for s in range(group):
        to = jnp.where(core_ref[0] == 0, s, s % side * side + s // side)
        into = pl.ds(pl.multiple_of(to * lines, 8), lines)
        for t in range(CUT // LANES):
            packed[t, into, :] = in_ref[s, :, t * LANES : (t + 1) * LANES].astype(jnp.float32)
    for k, out_ref in enumerate(out_refs):
        for i in range(each):
            for t in range(CUT // LANES):
                rows = [packed[t, pl.ds(r * cuts + k * each + i, group, stride=lines), :] for r in range(own)]
                at = i * CUT + t * LANES
                out_ref[:, at : at + LANES] = jnp.concatenate(rows, axis=0).astype(out_ref.dtype)


def unpack(core, packed, own):
    group, lines, _ = packed.shape
    out = jax.ShapeDtypeStruct((own * group, lines // own * CUT // PARTS), packed.dtype)
    return pl.pallas_call(
        functools.partial(unpack_kernel, own),
        out_shape=[out] * PARTS,
        in_specs=[SMEM, VMEM],
        out_specs=[VMEM] * PARTS,
        scratch_shapes=[pltpu.VMEM((CUT // LANES, group * lines, LANES), jnp.float32)],
        compiler_params=pltpu.CompilerParams(vmem_limit_bytes=24 << 20),
        name="unpack",
    )(core, packed)


def stage_kernel(first, core_ref, mine_ref, theirs_ref, out_ref, token_ref, sems):
    columns, width = mine_ref.shape[0], out_ref.shape[1]
    at = pl.multiple_of(core_ref[0] * columns, columns)
    other = pl.multiple_of((1 - core_ref[0]) * columns, columns)
    part = pl.ds(first, width)
    one = pltpu.make_async_copy(mine_ref.at[:, part], out_ref.at[pl.ds(at, columns)], sems.at[0])
    two = pltpu.make_async_copy(theirs_ref.at[:, part], out_ref.at[pl.ds(other, columns)], sems.at[1])
    one.start()
    two.start()
    token_ref[...] = jnp.zeros_like(token_ref)
    one.wait()
    two.wait()


def stage(core, mine, theirs, k):
    columns, width = mine.shape
    each = width // PARTS
    return pl.pallas_call(
        functools.partial(stage_kernel, k * each),
        out_shape=[pltpu.VMEM((2 * columns, each), mine.dtype), jax.ShapeDtypeStruct((8, LANES), jnp.float32)],
        in_specs=[SMEM, ANY, ANY],
        out_specs=[VMEM, VMEM],
        scratch_shapes=[pltpu.SemaphoreType.DMA((2,))],
        compiler_params=pltpu.CompilerParams(vmem_limit_bytes=2 << 20),
        cost_estimate=SMALL,
        name=f"stage{k}",
    )(core, pltpu.with_memory_space_constraint(mine, pltpu.HBM), pltpu.with_memory_space_constraint(theirs, pltpu.HBM))


def product_kernel(plan, group, side, *refs):
    final = group is not None
    outs = side if final else 1
    operands = 1 + max(max(line) for line in plan)
    a_refs = refs[:operands]
    tile_ref = refs[operands]
    rest = refs[operands + 1 :]
    sorting = 1 if final else 0
    at_ref, rest = (rest[0], rest[1:]) if final else (None, rest)
    scratch = 2 + sorting
    carried = rest[: len(rest) - outs - scratch]
    out_refs = rest[len(carried) : len(carried) + outs]
    rows, total = rest[len(carried) + outs :][:2]
    at = pl.program_id(0)
    high = rows.shape[0] // len(plan)

    for step in range(len(plan[0])):

        @pl.when(at == step)
        def _(step=step):
            for o, line in enumerate(plan):
                rows[o * high : (o + 1) * high, :] = a_refs[line[step]][...]

    def add(columns):
        return lax.dot_general(
            rows[...], tile_ref[:, columns], (((1,), (1,)), ((), ())), preferred_element_type=jnp.float32
        )

    columns = pl.ds(pl.multiple_of(at * STEP, STEP), STEP)

    @pl.when(at == 0)
    def _():
        total[...] = carried[0][...] + add(columns) if carried else add(columns)

    @pl.when(at > 0)
    def _():
        total[...] += add(columns)

    @pl.when(at == pl.num_programs(0) - 1)
    def _():
        if not final:
            out_refs[0][...] = total[...]
            return
        ordered = rest[-1]
        pieces = total.shape[0] // group
        height = ordered.shape[0] // group
        used = pieces * total.shape[1] // LANES
        for q in range(group):
            if used < height:
                ordered[q * height + used : (q + 1) * height, :] = jnp.zeros((height - used, LANES), jnp.float32)
        for t in range(total.shape[1] // LANES):
            for j in range(pieces):
                ordered[pl.ds(t * pieces + j, group, stride=height), :] = total[
                    j * group : (j + 1) * group, t * LANES : (t + 1) * LANES
                ]
        block = ordered.shape[0] // side
        for d, out_ref in zip(ways(side), out_refs):
            to = lax.rem(at_ref[0] + d, side)
            out_ref[...] = ordered[pl.ds(pl.multiple_of(to * block, block), block), :]


def ways(side):
    return [0] + sorted(range(1, side), key=lambda d: -min(d, side - d))


def padded(lines):
    return -(-lines // 8) * 8


def product(lines, tiles, carried=None, ends=None):
    operands, blocks, plan = [], [], []
    for line in lines:
        plan.append([])
        for step, (array, block) in enumerate(line):
            known = [i for i, other in enumerate(operands) if other is array]
            if known:
                blocks[known[0]][step] = block
            else:
                operands.append(array)
                blocks.append({step: block})
            plan[-1].append(known[0] if known else len(operands) - 1)
    high = operands[0].shape[0]
    steps = len(plan[0])
    columns = tiles.shape[0]
    rows = high * len(lines)

    def spec(used):
        low, top = min(used), max(used)
        base = used[low]
        return pl.BlockSpec((high, STEP), lambda s: (0, base + jnp.clip(s, low, top) - low))

    extra, specs = [], []
    group, side = None, None
    scratch = [pltpu.VMEM((rows, STEP), jnp.bfloat16), pltpu.VMEM((rows, columns), jnp.float32)]
    if ends is None:
        out, outs = (rows, columns), 1
    else:
        group, side, at = ends
        height = padded(rows // group * columns // LANES)
        out, outs = (group // side * height, LANES), side
        extra.append(at)
        specs.append(SMEM)
        scratch.append(pltpu.VMEM((group * height, LANES), jnp.float32))
    if carried is not None:
        extra.append(carried)
        specs.append(VMEM)
    made = pl.pallas_call(
        functools.partial(product_kernel, plan, group, side),
        grid=(steps,),
        out_shape=[jax.ShapeDtypeStruct(out, jnp.float32)] * outs,
        in_specs=[spec(used) for used in blocks] + [VMEM] + specs,
        out_specs=[pl.BlockSpec(out, lambda s: (0, 0))] * outs,
        scratch_shapes=scratch,
        compiler_params=pltpu.CompilerParams(vmem_limit_bytes=16 << 20),
        cost_estimate=SMALL,
        name=f"product{len(lines)}",
    )(*operands, tiles, *extra)
    return made[0] if ends is None else made


def middle_kernel(side, sizes, at_ref, *refs):
    in_refs, out_refs, totals = refs[: side * len(sizes)], refs[side * len(sizes) :][:side], refs[-len(sizes) :]
    for i, total in enumerate(totals):
        parts = in_refs[i * side : (i + 1) * side]
        summed = parts[0][...]
        for ref in parts[1:]:
            summed = summed + ref[...]
        total[...] = summed
    for d, out_ref in zip(ways(side), out_refs):
        to = lax.rem(at_ref[0] + d, side)
        base = 0
        for size, total in zip(sizes, totals):
            out_ref[base : base + size, :] = total[pl.ds(pl.multiple_of(to * size, 8), size), :]
            base += size


def middle(at, *groups):
    side = len(groups[0])
    sizes = tuple(parts[0].shape[0] // side for parts in groups)
    flat = [part for parts in groups for part in parts]
    return pl.pallas_call(
        functools.partial(middle_kernel, side, sizes),
        out_shape=[jax.ShapeDtypeStruct((sum(sizes), LANES), jnp.float32)] * side,
        in_specs=[SMEM] + [VMEM] * len(flat),
        out_specs=[VMEM] * side,
        scratch_shapes=[pltpu.VMEM((size * side, LANES), jnp.float32) for size in sizes],
        compiler_params=pltpu.CompilerParams(vmem_limit_bytes=16 << 20),
        cost_estimate=SMALL,
        name="middle",
    )(at, *flat)


def total_kernel(own, side, groups, plan, *refs):
    in_refs, out_refs, total, blocks = refs[:side], refs[side:-2], refs[-2], refs[-1]
    summed = in_refs[0][...]
    for ref in in_refs[1:]:
        summed = summed + ref[...]
    total[...] = summed
    blocks[...] = jnp.zeros_like(blocks)
    base = 0
    for steps, tall in groups:
        pieces = own * len(steps)
        for o, step in enumerate(steps):
            for t in range(tall // pieces):
                at = base + t * pieces + o * own
                blocks[step, t * own : (t + 1) * own, :] = total[at : at + own, :]
        base += tall
    for out_ref, steps in zip(out_refs, plan):
        for i, step in enumerate(steps):
            out_ref[i] = blocks[step].astype(out_ref.dtype)


def totals(parts, own, groups, plan, columns):
    count = sum(len(steps) for steps, _ in groups)
    height = -(-own * columns // LANES // 16) * 16
    return pl.pallas_call(
        functools.partial(total_kernel, own, len(parts), groups, plan),
        out_shape=[jax.ShapeDtypeStruct((len(steps), height, LANES), jnp.bfloat16) for steps in plan],
        in_specs=[VMEM] * len(parts),
        out_specs=[VMEM] * len(plan),
        scratch_shapes=[pltpu.VMEM(parts[0].shape, jnp.float32), pltpu.VMEM((count, height, LANES), jnp.float32)],
        compiler_params=pltpu.CompilerParams(vmem_limit_bytes=16 << 20),
        cost_estimate=SMALL,
        name="totals",
    )(*parts)


def unique(blocks):
    arrays = []
    for array, _ in blocks:
        if not any(array is other for other in arrays):
            arrays.append(array)
    return arrays, [([i for i, other in enumerate(arrays) if other is array][0], at) for array, at in blocks]


def gather_kernel(plan, *refs):
    for i, (n, at) in enumerate(plan):
        refs[-1][i] = refs[n][at]


def gather(blocks):
    arrays, plan = unique(blocks)
    return pl.pallas_call(
        functools.partial(gather_kernel, plan),
        out_shape=jax.ShapeDtypeStruct((len(blocks),) + arrays[0].shape[1:], arrays[0].dtype),
        in_specs=[VMEM] * len(arrays),
        out_specs=VMEM,
        compiler_params=pltpu.CompilerParams(vmem_limit_bytes=16 << 20),
        cost_estimate=SMALL,
        name="gather",
    )(*arrays)


def place_kernel(plan, width, chip_ref, *refs):
    out_ref = refs[-1]
    own, count = out_ref.shape[0], len(plan)
    for step, (n, at) in enumerate(plan):
        source = lax.rem(chip_ref[0] - step + count, count)
        block = refs[n][at].astype(jnp.float32)
        row = [block[t * own : (t + 1) * own, :] for t in range(width // LANES)]
        into = pl.ds(pl.multiple_of(source * width, LANES), width)
        out_ref[:, into] = jnp.concatenate(row, axis=1).astype(out_ref.dtype)


def place(chip, blocks, own, width):
    arrays, plan = unique(blocks)
    return pl.pallas_call(
        functools.partial(place_kernel, plan, width),
        out_shape=jax.ShapeDtypeStruct((own, width * len(blocks)), jnp.bfloat16),
        in_specs=[SMEM] + [VMEM] * len(arrays),
        out_specs=VMEM,
        compiler_params=pltpu.CompilerParams(vmem_limit_bytes=16 << 20),
        cost_estimate=SMALL,
        name="place",
    )(chip, *arrays)


def after(x, *done):
    return lax.optimization_barrier((x,) + done)[0]


def local(amplitudes, integrals, screen, live, owner):
    own = amplitudes.shape[0]
    row_count = lax.axis_size("row")
    pairs = lax.axis_size("pair")
    chips = row_count // 2
    last = chips // 2
    row = lax.axis_index("row").astype(jnp.int32)
    core, chip = (row % 2).reshape(1), (row // 2).reshape(1)
    side = math.isqrt(pairs)
    pair = lax.axis_index("pair").astype(jnp.int32)
    slow = jnp.where(core == 0, pair // side, pair % side)
    fast = jnp.where(core == 0, pair % side, pair // side)

    def along(x, d):
        return lax.ppermute(x, "row", [(2 * z + c, 2 * ((z + d) % chips) + c) for z in range(chips) for c in range(2)])

    def shifted(x, d, slow):
        moves = []
        for p in range(pairs):
            over_x = p % side + (p // side + d) % side * side
            over_y = p // side * side + (p % side + d) % side
            for r in range(row_count):
                to = over_x if (r % 2 == 0) == slow else over_y
                moves.append((p * row_count + r, to * row_count + r))
        return lax.ppermute(x, ("pair", "row"), moves)

    mine = integrals[0]
    theirs = lax.ppermute(mine, "row", [(r, r ^ 1) for r in range(row_count)])
    columns = 2 * mine.shape[0]
    packed, core, chip, slow, fast = lax.optimization_barrier(
        (pick(amplitudes, screen, live, owner), core, chip, slow, fast)
    )
    start = unpack(core, lax.all_to_all(packed, "pair", split_axis=0, concat_axis=0, tiled=True), own)

    tiles, tokens = zip(*[stage(core, mine, theirs, k) for k in range(PARTS)])
    per = start[0].shape[1] // STEP
    half = per // 2 * STEP
    forward, backward = list(start), list(start)

    def whole(array):
        return [(array, b) for b in range(per)]

    def on(k, *done):
        forward[k] = along(after(forward[k], *done) if done else forward[k], 1)
        backward[k] = along(after(backward[k], *done) if done else backward[k], -1)

    def chain(k, lines, carried):
        ends = (pairs, side, slow) if k == PARTS - 1 else None
        return product(lines, tiles[k], carried, ends)

    def over_slow(parts):
        return [parts[0]] + [shifted(part, d, True) for part, d in zip(parts[1:], ways(side)[1:])]

    def over_fast(parts):
        return [parts[0]] + [shifted(part, d, False) for part, d in zip(parts[1:], ways(side)[1:])]

    near, made = [[whole(start[k])] for k in range(PARTS)], []
    for hop in range(1, last - 1):
        for k in range(PARTS):
            on(k, *([tokens[k]] if hop == last - 2 else []))
            near[k] += [whole(forward[k]), whole(backward[k])]
    for k in range(PARTS):
        made.append(chain(k, near[k], made[-1] if made else None))
    near_steps = (0,) + tuple(d % chips for hop in range(1, last - 1) for d in (-hop, hop))
    on(0)
    on(1, made[0])
    near_parts = over_slow(made[-1])
    far, ended = [], None
    for k in range(PARTS):
        low = along(after(forward[k][:, :half], made[-1][0]), 1)
        high = along(after(backward[k][:, half:], made[-1][0]), -1)
        far.append([whole(forward[k]), whole(backward[k]), [(low, 0), (high, 0)]])
    for k in range(PARTS):
        if k == PARTS - 1:
            ended = after(ended, *near_parts)
        ended = chain(k, far[k], ended)
    far_steps = ((1 - last) % chips, last - 1, last)
    groups = tuple((steps, padded(own * len(steps) * columns // LANES)) for steps in (near_steps, far_steps))
    plan = (far_steps[::-1], (0,), (1, 2), (chips - 1, chips - 2))
    parts = over_fast(middle(fast, near_parts, over_slow(ended)))
    distant, here, right, left = totals(parts, own, groups, plan, columns)
    distant, right, left = along(distant, last), along(right, 1), along(left, -1)
    right_two = along(gather([(right, 1), (distant, plan[0].index(last + 1))]), 1)
    left_two = along(gather([(left, 1), (distant, plan[0].index(last - 1))]), -1)
    blocks = {
        0: (here, 0),
        1: (right, 0),
        2: (right_two, 0),
        last - 1: (left_two, 1),
        last: (distant, plan[0].index(last)),
        last + 1: (right_two, 1),
        chips - 2: (left_two, 0),
        chips - 1: (left, 0),
    }
    return place(chip, [blocks[s] for s in range(chips)], own, columns)


def solution(mesh):
    return jax.shard_map(
        local,
        mesh=mesh,
        in_specs=(
            P(("pair", "row"), None, None),
            P("pair", "row", None),
            P(("pair", "row"), None),
            P(),
            P(),
        ),
        out_specs=P(("pair", "row"), None),
        check_vma=False,
    )
```
